32 devices in a mesh: mol: 2 (over x), occ: 16 (over z, y, core).
Axes of the slice: x: 2, y: 2, z: 4, core: 2. Of those that a mesh axis runs over, the one named last changes fastest.
Arguments:
- amplitudes: bfloat16 [256, 16, 64, 64], P(('mol', 'occ')), parts along dimension 0, may hold values from -0.16699219 to 0.16699219
- lambdas: bfloat16 [256, 16, 64, 64], P(('mol', 'occ')), parts along dimension 0, may hold values from -6 to 6
- pair_list: int32 [256, 2], P(('mol', 'occ')), parts along dimension 0, may hold values from 0 to 299
- tile_list: int32 [16, 2], replicated, may hold values from 0 to 37
- occ_energy: float32 [600], P('mol'), parts along dimension 0, may hold values from -2 to -0.5
- vir_energy: float32 [4864], P('mol'), parts along dimension 0, may hold values from 0.5 to 3
Outputs:
- new_lambdas: bfloat16 [256, 16, 64, 64], P(('mol', 'occ')), parts along dimension 0
The draws below stay inside these ranges and needn't reach their ends.
There are 2 independent parts, one for each index of `mol`. The reference program is written for one: setup_inputs(seed, part) draws one part's arguments, and reference() takes and returns one part's arrays. A program takes and returns all parts, laid end to end along the dimension named above; an argument that names none is the same for every part. Nothing has to cross between parts.
All inputs are finite; a program needn't handle non-finite values.
Results may differ from the reference program's by a relative error of at most 0.0075.
Values may be sent and summed in bfloat16 or wider, within the bound.
A program may use at most 128 MiB of HBM per device.

```python
import jax
import jax.numpy as jnp
from jax import lax

TILE = 64
NVT = 38
NOCC = 300
NPAIR = 128
NNZ = 16


def plant(drawn, rng, low, top_value):
    longest = drawn.shape.index(max(drawn.shape))
    spots = []
    for shift in (0, 1):
        where = [jax.random.randint(jax.random.fold_in(rng, axis), (), 0, length) for axis, length in enumerate(drawn.shape)]
        where[longest] = (where[longest] + shift) % drawn.shape[longest]
        spots.append(tuple(where))
    return drawn.at[spots[0]].set(low).at[spots[1]].set(top_value)


def spiked(values, rng, source, target, blocks, factor):
    def block_of(dim):
        return (jnp.arange(values.shape[dim]) // (values.shape[dim] // blocks)).reshape((-1,) + (1,) * (values.ndim - 1 - dim))

    one_side = jax.random.permutation(rng, blocks)[block_of(target)]
    second = (block_of(target) + blocks // 2) % blocks
    return jnp.where((block_of(source) == one_side) | (block_of(source) == second), factor * values, values)


def levels(own_key, extent, pieces, least, largest):
    gain = 1.0
    for axis_at, shards_of in pieces:
        heights = jax.random.uniform(jax.random.fold_in(jax.random.fold_in(own_key, 6), axis_at), (shards_of,), jnp.float32, least / len(pieces), largest / len(pieces))
        gain = gain * jnp.repeat(jnp.exp(heights), extent[axis_at] // shards_of).reshape((-1,) + (1,) * (len(extent) - 1 - axis_at))
    return gain


def bell_draw(own_key, extent, scale, limit, split=(), dtype=jnp.bfloat16):
    values = scale * jax.random.normal(own_key, extent, jnp.float32)
    if split:
        values = values * levels(own_key, extent, split, -0.22, 0.18)
    return jnp.clip(values, -limit, limit).astype(dtype)


def noise_with(rng, shape, spread, reach, split, heavy, kind=jnp.bfloat16):
    array = spread * jax.random.normal(rng, shape, jnp.float32)
    if split:
        array = array * levels(rng, shape, split, -0.22, 0.18)
    return jnp.clip(spiked(array, jax.random.fold_in(rng, 3), *heavy), -reach, reach).astype(kind)


def setup_inputs(seed: int = 0, part: int = 0) -> dict:
    streams_of = jax.random.split(jax.random.key(seed), 7)
    part_keys = jax.random.split(jax.random.fold_in(streams_of[6], part), 7)
    return {
        "amplitudes": noise_with(part_keys[0], (NPAIR, NNZ, TILE, TILE), (1.5 * (NNZ * NPAIR) ** -0.25 * TILE ** -0.5), 0.16699219, ((0, 16),), (1, 0, 16, 2.0)),
        "lambdas": bell_draw(part_keys[1], (NPAIR, NNZ, TILE, TILE), 1.0, 6.0, ((0, 16),)),
        "pair_list": plant(jax.random.randint(part_keys[2], (NPAIR, 2), 0, NOCC), jax.random.fold_in(part_keys[2], 1), 0, NOCC - 1).astype(jnp.int32),
        "tile_list": plant(jax.random.randint(streams_of[3], (NNZ, 2), 0, NVT), jax.random.fold_in(streams_of[3], 1), 0, NVT - 1).astype(jnp.int32),
        "occ_energy": jnp.clip(jax.random.uniform(part_keys[4], (NOCC,), jnp.float32, -2.0, -0.5), -2.0, -0.5),
        "vir_energy": jnp.clip(jax.random.uniform(part_keys[5], (NVT * TILE,), jnp.float32, 0.5, 3.0), 0.5, 3.0),
    }


def reference(amplitudes, lambdas, pair_list, tile_list, occ_energy, vir_energy):
    rows = amplitudes.shape[0]
    amp_flat = amplitudes.reshape(rows, -1)
    lam_flat = lambdas.reshape(rows, -1)
    intersection = lax.dot_general(amp_flat, lam_flat, (((1,), (1,)), ((), ())), preferred_element_type=jnp.float32)
    intersection_b = intersection.astype(jnp.bfloat16)
    ladder = (0.5 * jnp.dot(intersection_b, amp_flat, preferred_element_type=jnp.float32)).astype(jnp.bfloat16)
    ladder = ladder.reshape(amplitudes.shape)
    vir_tiles = vir_energy.reshape(NVT, TILE)
    first_vir = vir_tiles[tile_list[:, 0]]
    second_vir = vir_tiles[tile_list[:, 1]]
    occ_first = occ_energy[pair_list[:, 0]]
    occ_second = occ_energy[pair_list[:, 1]]
    denom = first_vir[None, :, :, None] + second_vir[None, :, None, :] - occ_first[:, None, None, None] - occ_second[:, None, None, None]
    total = lambdas.astype(jnp.float32) + ladder.astype(jnp.float32)
    return (total / denom).astype(jnp.bfloat16)
```

```python
import functools

import jax
import jax.numpy as jnp
from jax import lax
from jax.experimental import pallas as pl
from jax.experimental.pallas import tpu as pltpu
from jax.sharding import PartitionSpec as P

F32 = jnp.float32
BF16 = jnp.bfloat16
HELD = 8
ROWS = 256
FOLD = 32


def fold_tile(x):
    return jnp.concatenate([x[:, :FOLD, :], x[:, FOLD:, :]], axis=-1)


def kernel(
    n, groups, nt,
    tiles_ref, pairs_ref, occ_ref, vir_ref, amp_hbm, lam_hbm,
    out_hbm,
    amp, lam, pt, plam, lamh, tbuf, lbuf, lad, ladr, dscr, gacc, asend, arecv, bsend, brecv, kmat,
    in_sem, t_send, t_recv, l_send, l_recv, a_send, a_recv, b_send, b_recv, d_send, d_recv, o_sem,
):
    cols = n // groups
    per = nt // cols
    me = lax.axis_index("occ")
    c = me % cols
    first = (me // cols) * cols

    def chunk(k):
        return lax.rem(c + k, cols)

    def load(which, src, dst, cc):
        span = pl.ds(cc * per, per)
        return pltpu.make_async_copy(src.at[:, span], dst.at[:, span], in_sem.at[which, cc])

    def load_start(k, _):
        load(0, amp_hbm, amp, chunk(k)).start()
        load(1, lam_hbm, lam, chunk(k)).start()
        return 0

    lax.fori_loop(0, cols, load_start, 0)

    barrier = pltpu.get_barrier_semaphore()

    def greet(k, _):
        pl.semaphore_signal(
            barrier, inc=1, device_id={"occ": lax.rem(me + k, n)}, device_id_type=pl.DeviceIdType.MESH
        )
        return 0

    lax.fori_loop(1, n, greet, 0)

    r_id = lax.broadcasted_iota(jnp.int32, (ROWS, ROWS), 0)
    m_id = lax.broadcasted_iota(jnp.int32, (ROWS, ROWS), 1)
    pack_m = ((r_id % HELD) * FOLD + r_id // HELD == m_id).astype(BF16)
    unpack_m = ((m_id % HELD) * FOLD + m_id // HELD == r_id).astype(BF16)

    def pack(cc):
        load(0, amp_hbm, amp, cc).wait()
        load(1, lam_hbm, lam, cc).wait()
        for i in range(per):
            s = cc * per + i
            t = fold_tile(amp[:, s]).reshape(ROWS, 2 * 64)
            pt[s] = jnp.dot(pack_m, t, preferred_element_type=F32).astype(BF16)
            u = fold_tile(lam[:, s]).reshape(ROWS, 2 * 64)
            lamh[s] = u
            plam[s] = jnp.dot(pack_m, u, preferred_element_type=F32).astype(BF16)

    def rcopy(src, dst, send, recv, peer):
        return pltpu.make_async_remote_copy(
            src_ref=src, dst_ref=dst, send_sem=send, recv_sem=recv,
            device_id={"occ": peer}, device_id_type=pl.DeviceIdType.MESH,
        )

    def send_t(peer):
        span = pl.ds(lax.rem(peer, cols) * per, per)
        return rcopy(pt.at[span], tbuf.at[me], t_send.at[peer], t_recv.at[me], peer)

    def send_l(cc):
        return rcopy(plam.at[pl.ds(cc * per, per)], lbuf.at[c], l_send.at[cc], l_recv.at[c], first + cc)

    def wait_t(src):
        rcopy(pt.at[pl.ds(0, per)], tbuf.at[src], t_send.at[src], t_recv.at[src], src).wait_recv()

    def wait_l(cc):
        rcopy(plam.at[pl.ds(0, per)], lbuf.at[cc], l_send.at[cc], l_recv.at[cc], first + cc).wait_recv()

    pack(c)
    pl.semaphore_wait(barrier, n - 1)
    for g in range(1, groups):
        send_t(lax.rem(me + g * cols, n)).start()

    def pack_send(k, _):
        cc = chunk(k)
        pack(cc)
        for g in range(groups - 1, -1, -1):
            send_t(lax.rem(first + g * cols, n) + cc).start()
        send_l(cc).start()
        return 0

    lax.fori_loop(1, cols, pack_send, 0)
    tbuf[me] = pt[pl.ds(c * per, per)]
    lbuf[c] = plam[pl.ds(c * per, per)]

    def energies(s, _):
        one = vir_ref[pl.ds(tiles_ref[s, 0], 1), :]
        two = vir_ref[pl.ds(tiles_ref[s, 1], 1), :]
        d = jnp.transpose(jnp.broadcast_to(one, (64, 64))) + two
        dscr[s] = jnp.concatenate([d[:FOLD], d[FOLD:]], axis=-1)
        return 0

    lax.fori_loop(0, nt, energies, 0)

    def arrive_t(k, _):
        wait_t(lax.rem(me + n - k, n))
        return 0

    def arrive_l(k, _):
        wait_l(lax.rem(c + cols - k, cols))
        return 0

    lax.fori_loop(1, cols, arrive_l, 0)
    lax.fori_loop(1, n, arrive_t, 0)

    def two_rows(ref, lo, count, t, g):
        a = ref[pl.ds(lo, count), t, pl.ds(g * 32, 16), :].reshape(count * 16, 128)
        b = ref[pl.ds(lo, count), t, pl.ds(g * 32 + 16, 16), :].reshape(count * 16, 128)
        return jnp.concatenate([a, b], axis=-1)

    gacc[...] = jnp.zeros_like(gacc)
    for t in range(per):
        def gram(g, _):
            y = two_rows(lbuf, 0, cols, t, g)
            for lo in range(0, n, 16):
                x = two_rows(tbuf, lo, 16, t, g)
                gacc[pl.ds(lo * 16, 256), :] += lax.dot_general(
                    x, y, (((1,), (1,)), ((), ())), preferred_element_type=F32
                )
            return 0

        lax.fori_loop(0, ROWS // 32, gram, 0, unroll=4 if n <= 16 else 1)

    width = cols * 16
    odd = (lax.broadcasted_iota(jnp.int32, (HELD, width), 1) // HELD) % 2

    def fold_gram(i, _):
        lo = gacc[pl.ds(i * 16, HELD), :]
        hi = gacc[pl.ds(i * 16 + HELD, HELD), :]
        asend[i] = jnp.where(odd == 0, lo, hi)
        return 0

    lax.fori_loop(0, n, fold_gram, 0, unroll=4)

    def send_a(peer):
        return rcopy(asend.at[peer], arecv.at[me], a_send.at[peer], a_recv.at[me], peer)

    def start_a(k, _):
        send_a(lax.rem(me + k, n)).start()
        return 0

    lax.fori_loop(1, n, start_a, 0)
    arecv[me] = asend[me]

    def arrive_a(k, _):
        src = lax.rem(me + n - k, n)
        rcopy(asend.at[src], arecv.at[src], a_send.at[src], a_recv.at[src], src).wait_recv()
        return 0

    lax.fori_loop(1, n, arrive_a, 0)
    for g in range(groups):
        total = arecv[g * cols]
        for i in range(1, cols):
            total = total + arecv[g * cols + i]
        other = jnp.where(odd == 0, pltpu.roll(total, width - HELD, 1), pltpu.roll(total, HELD, 1))
        rounded = (total + other).astype(BF16).astype(F32)
        bsend[:, g * width:(g + 1) * width] = 0.5 * rounded

    def send_b(cc):
        return rcopy(bsend, brecv.at[c], b_send.at[cc], b_recv.at[c], first + cc)

    def start_b(k, _):
        send_b(chunk(k)).start()
        return 0

    lax.fori_loop(1, cols, start_b, 0)
    brecv[c] = bsend[...]

    def arrive_b(k, _):
        cc = lax.rem(c + cols - k, cols)
        rcopy(bsend, brecv.at[cc], b_send.at[cc], b_recv.at[cc], first + cc).wait_recv()
        return 0

    lax.fori_loop(1, cols, arrive_b, 0)
    all_odd = (lax.broadcasted_iota(jnp.int32, (HELD, n * 16), 1) // HELD) % 2

    def expand(i, _):
        rows = brecv[i]
        both = jnp.concatenate(
            [jnp.where(all_odd == 0, rows, 0.0), jnp.where(all_odd == 1, rows, 0.0)], axis=0
        )
        kmat[pl.ds(i * 16, 16), :] = both.astype(BF16)
        return 0

    lax.fori_loop(0, cols, expand, 0, unroll=4)

    def send_d(cc, t):
        return rcopy(lad.at[cc, t], ladr.at[c, t], d_send.at[cc, t], d_recv.at[c, t], first + cc)

    for t in range(per):
        def ladder(g, _):
            x = two_rows(tbuf, 0, n, t, g)
            y = jnp.dot(kmat[...], x, preferred_element_type=F32).astype(BF16)
            lad[:, t, pl.ds(g * 32, 16), :] = y[:, :128].reshape(cols, 16, 128)
            lad[:, t, pl.ds(g * 32 + 16, 16), :] = y[:, 128:].reshape(cols, 16, 128)
            return 0

        lax.fori_loop(0, ROWS // 32, ladder, 0, unroll=4 if n <= 16 else 1)

        def start_d(k, _):
            send_d(chunk(k), t).start()
            return 0

        lax.fori_loop(1, cols, start_d, 0)
    ladr[c] = lad[c]

    def store(cc):
        span = pl.ds(cc * per, per)
        return pltpu.make_async_copy(amp.at[:, span], out_hbm.at[:, span], o_sem.at[cc])

    def finish(cc):
        for t in range(per):
            s = cc * per + t
            z = jnp.dot(unpack_m, ladr[cc, t], preferred_element_type=F32)
            total = lamh[s].astype(F32) + z
            d = dscr[s]
            for p in range(HELD):
                e = d - occ_ref[pairs_ref[p, 0]] - occ_ref[pairs_ref[p, 1]]
                q = total[p * FOLD:(p + 1) * FOLD] / e
                amp[p, s, :FOLD, :] = q[:, :64].astype(BF16)
                amp[p, s, FOLD:, :] = q[:, 64:].astype(BF16)
        store(cc).start()

    finish(c)

    def arrive_d(k, _):
        cc = lax.rem(c + cols - k, cols)
        for t in range(per):
            rcopy(
                lad.at[cc, t], ladr.at[cc, t], d_send.at[cc, t], d_recv.at[cc, t], first + cc
            ).wait_recv()
        finish(cc)
        return 0

    lax.fori_loop(1, cols, arrive_d, 0)

    def drain_n(k, _):
        peer = lax.rem(me + k, n)
        send_t(peer).wait_send()
        send_a(peer).wait_send()
        return 0

    lax.fori_loop(1, n, drain_n, 0)

    def drain_c(k, _):
        cc = chunk(k)
        send_l(cc).wait_send()
        send_b(cc).wait_send()
        for t in range(per):
            send_d(cc, t).wait_send()
        return 0

    lax.fori_loop(1, cols, drain_c, 0)

    def drain_out(k, _):
        store(k).wait()
        return 0

    lax.fori_loop(0, cols, drain_out, 0)


def shards(n, amplitudes, lambdas, pair_list, tile_list, occ_energy, vir_energy):
    nt = amplitudes.shape[1]
    groups = 2
    cols = n // groups
    per = nt // cols
    packed = (nt, ROWS, 128)
    dma = pltpu.SemaphoreType.DMA
    smem = pl.BlockSpec(memory_space=pltpu.SMEM)
    vmem = pl.BlockSpec(memory_space=pltpu.VMEM)
    hbm = pl.BlockSpec(memory_space=pl.ANY)
    return pl.pallas_call(
        functools.partial(kernel, n, groups, nt),
        out_shape=jax.ShapeDtypeStruct(lambdas.shape, BF16),
        in_specs=[smem, smem, smem, vmem, hbm, hbm],
        out_specs=hbm,
        scratch_shapes=[
            pltpu.VMEM(amplitudes.shape, BF16),
            pltpu.VMEM(lambdas.shape, BF16),
            pltpu.VMEM(packed, BF16),
            pltpu.VMEM(packed, BF16),
            pltpu.VMEM(packed, BF16),
            pltpu.VMEM((n, per, ROWS, 128), BF16),
            pltpu.VMEM((cols, per, ROWS, 128), BF16),
            pltpu.VMEM((cols, per, ROWS, 128), BF16),
            pltpu.VMEM((cols, per, ROWS, 128), BF16),
            pltpu.VMEM((nt, FOLD, 128), F32),
            pltpu.VMEM((n * 16, cols * 16), F32),
            pltpu.VMEM((n, HELD, cols * 16), F32),
            pltpu.VMEM((n, HELD, cols * 16), F32),
            pltpu.VMEM((HELD, n * 16), F32),
            pltpu.VMEM((cols, HELD, n * 16), F32),
            pltpu.VMEM((cols * 16, n * 16), BF16),
            dma((2, cols)),
            dma((n,)), dma((n,)),
            dma((cols,)), dma((cols,)),
            dma((n,)), dma((n,)),
            dma((cols,)), dma((cols,)),
            dma((cols, per)), dma((cols, per)),
            dma((cols,)),
        ],
        compiler_params=pltpu.CompilerParams(
            collective_id=0,
            has_side_effects=True,
            vmem_limit_bytes=(32 if n <= 16 else 61) * 2**20,
        ),
    )(tile_list, pair_list, occ_energy, vir_energy.reshape(-1, 64), amplitudes, lambdas)


def solution(mesh):
    return jax.shard_map(
        functools.partial(shards, mesh.shape["occ"]),
        mesh=mesh,
        in_specs=(
            P(("mol", "occ"), None, None, None),
            P(("mol", "occ"), None, None, None),
            P(("mol", "occ"), None),
            P(),
            P("mol"),
            P("mol"),
        ),
        out_specs=P(("mol", "occ"), None, None, None),
        check_vma=False,
    )
```

```python
import functools

import jax
import jax.numpy as jnp
from jax import lax
from jax.experimental import pallas as pl
from jax.experimental.pallas import tpu as pltpu
from jax.sharding import PartitionSpec as P

F32 = jnp.float32
BF16 = jnp.bfloat16
HELD = 8
ROWS = 256
FOLD = 32


def fold_tile(x):
    return jnp.concatenate([x[:, :FOLD, :], x[:, FOLD:, :]], axis=-1)


def kernel(
    n, groups, nt,
    tiles_ref, pairs_ref, occ_ref, vir_ref, amp_hbm, lam_hbm,
    out_hbm,
    amp, lam, pt, plam, lamh, tbuf, lbuf, lad, ladr, dscr, gacc, asend, arecv, bsend, brecv, kmat,
    in_sem, t_send, t_recv, l_send, l_recv, a_send, a_recv, b_send, b_recv, d_send, d_recv, o_sem,
):
    cols = n // groups
    per = nt // cols
    me = lax.axis_index("occ")
    c = me % cols
    first = (me // cols) * cols

    def chunk(k):
        return lax.rem(c + k, cols)

    def load(which, src, dst, s):
        return pltpu.make_async_copy(src.at[:, s], dst.at[:, s], in_sem.at[which, s])

    def load_start(k, _):
        s = chunk(k % cols) * per + k // cols
        load(0, amp_hbm, amp, s).start()
        load(1, lam_hbm, lam, s).start()
        return 0

    lax.fori_loop(0, nt, load_start, 0)

    barrier = pltpu.get_barrier_semaphore()

    def greet(k, _):
        pl.semaphore_signal(
            barrier, inc=1, device_id={"occ": lax.rem(me + k, n)}, device_id_type=pl.DeviceIdType.MESH
        )
        return 0

    lax.fori_loop(1, n, greet, 0)

    r_id = lax.broadcasted_iota(jnp.int32, (ROWS, ROWS), 0)
    m_id = lax.broadcasted_iota(jnp.int32, (ROWS, ROWS), 1)
    pack_m = ((r_id % HELD) * FOLD + r_id // HELD == m_id).astype(BF16)
    unpack_m = ((m_id % HELD) * FOLD + m_id // HELD == r_id).astype(BF16)

    def pack(s):
        load(0, amp_hbm, amp, s).wait()
        load(1, lam_hbm, lam, s).wait()
        t = fold_tile(amp[:, s]).reshape(ROWS, 2 * 64)
        pt[s] = jnp.dot(pack_m, t, preferred_element_type=F32).astype(BF16)
        u = fold_tile(lam[:, s]).reshape(ROWS, 2 * 64)
        lamh[s] = u
        plam[s] = jnp.dot(pack_m, u, preferred_element_type=F32).astype(BF16)

    def rcopy(src, dst, send, recv, peer):
        return pltpu.make_async_remote_copy(
            src_ref=src, dst_ref=dst, send_sem=send, recv_sem=recv,
            device_id={"occ": peer}, device_id_type=pl.DeviceIdType.MESH,
        )

    def send_t(peer, t):
        s = lax.rem(peer, cols) * per + t
        return rcopy(pt.at[s], tbuf.at[me, t], t_send.at[peer, t], t_recv.at[me, t], peer)

    def send_l(cc, t):
        s = cc * per + t
        return rcopy(plam.at[s], lbuf.at[c, t], l_send.at[cc, t], l_recv.at[c, t], first + cc)

    def wait_t(src, t):
        rcopy(pt.at[0], tbuf.at[src, t], t_send.at[src, t], t_recv.at[src, t], src).wait_recv()

    def wait_l(cc, t):
        rcopy(plam.at[0], lbuf.at[cc, t], l_send.at[cc, t], l_recv.at[cc, t], first + cc).wait_recv()

    pack(c * per)
    pl.semaphore_wait(barrier, n - 1)
    for t in range(per):
        if t > 0:
            pack(c * per + t)
        for g in range(1, groups):
            send_t(lax.rem(me + g * cols, n), t).start()

        def pack_send(k, _):
            cc = chunk(k)
            pack(cc * per + t)
            for g in range(groups - 1, -1, -1):
                send_t(lax.rem(first + g * cols, n) + cc, t).start()
            send_l(cc, t).start()
            return 0

        lax.fori_loop(1, cols, pack_send, 0)
    tbuf[me] = pt[pl.ds(c * per, per)]
    lbuf[c] = plam[pl.ds(c * per, per)]

    def vir_tile(i):
        row = vir_ref[pl.ds(i // 2, 1), :]
        return jnp.where(i % 2 == 0, row[:, :64], row[:, 64:])

    def energies(s, _):
        one = vir_tile(tiles_ref[0, s])
        two = vir_tile(tiles_ref[1, s])
        d = jnp.transpose(jnp.broadcast_to(one, (64, 64))) + two
        dscr[s] = jnp.concatenate([d[:FOLD], d[FOLD:]], axis=-1)
        return 0

    lax.fori_loop(0, nt, energies, 0)

    def two_rows(ref, lo, count, t, g):
        a = ref[pl.ds(lo, count), t, pl.ds(g * 32, 16), :].reshape(count * 16, 128)
        b = ref[pl.ds(lo, count), t, pl.ds(g * 32 + 16, 16), :].reshape(count * 16, 128)
        return jnp.concatenate([a, b], axis=-1)

    for t in range(per):
        def arrive_t(k, _):
            wait_t(lax.rem(me + n - k, n), t)
            return 0

        def arrive_l(k, _):
            wait_l(lax.rem(c + cols - k, cols), t)
            return 0

        lax.fori_loop(1, cols, arrive_l, 0)
        lax.fori_loop(1, n, arrive_t, 0)

        def gram(i, _):
            acc = None
            for g in range(ROWS // 32):
                x = two_rows(tbuf, i * 16, 16, t, g)
                y = two_rows(lbuf, 0, cols, t, g)
                term = lax.dot_general(x, y, (((1,), (1,)), ((), ())), preferred_element_type=F32)
                acc = term if acc is None else acc + term
            rows = pl.ds(i * 256, 256)
            gacc[rows, :] = acc if t == 0 else gacc[rows, :] + acc
            return 0

        lax.fori_loop(0, n // 16, gram, 0)

    width = cols * 16
    odd = (lax.broadcasted_iota(jnp.int32, (HELD, width), 1) // HELD) % 2

    def fold_gram(i, _):
        lo = gacc[pl.ds(i * 16, HELD), :]
        hi = gacc[pl.ds(i * 16 + HELD, HELD), :]
        asend[i] = jnp.where(odd == 0, lo, hi)
        return 0

    lax.fori_loop(0, n, fold_gram, 0, unroll=4)

    def send_a(peer):
        return rcopy(asend.at[peer], arecv.at[me], a_send.at[peer], a_recv.at[me], peer)

    def start_a(k, _):
        send_a(lax.rem(me + k, n)).start()
        return 0

    lax.fori_loop(1, n, start_a, 0)
    arecv[me] = asend[me]

    def arrive_a(k, _):
        src = lax.rem(me + n - k, n)
        rcopy(asend.at[src], arecv.at[src], a_send.at[src], a_recv.at[src], src).wait_recv()
        return 0

    lax.fori_loop(1, n, arrive_a, 0)
    for g in range(groups):
        total = arecv[g * cols]
        for i in range(1, cols):
            total = total + arecv[g * cols + i]
        other = jnp.where(odd == 0, pltpu.roll(total, width - HELD, 1), pltpu.roll(total, HELD, 1))
        rounded = (total + other).astype(BF16).astype(F32)
        bsend[:, g * width:(g + 1) * width] = 0.5 * rounded

    def send_b(cc):
        return rcopy(bsend, brecv.at[c], b_send.at[cc], b_recv.at[c], first + cc)

    def start_b(k, _):
        send_b(chunk(k)).start()
        return 0

    lax.fori_loop(1, cols, start_b, 0)
    brecv[c] = bsend[...]

    def arrive_b(k, _):
        cc = lax.rem(c + cols - k, cols)
        rcopy(bsend, brecv.at[cc], b_send.at[cc], b_recv.at[cc], first + cc).wait_recv()
        return 0

    lax.fori_loop(1, cols, arrive_b, 0)
    all_odd = (lax.broadcasted_iota(jnp.int32, (HELD, n * 16), 1) // HELD) % 2

    def expand(i, _):
        rows = brecv[i]
        both = jnp.concatenate(
            [jnp.where(all_odd == 0, rows, 0.0), jnp.where(all_odd == 1, rows, 0.0)], axis=0
        )
        kmat[pl.ds(i * 16, 16), :] = both.astype(BF16)
        return 0

    lax.fori_loop(0, cols, expand, 0, unroll=8)

    def send_d(cc, t):
        return rcopy(lad.at[cc, t], ladr.at[c, t], d_send.at[cc, t], d_recv.at[c, t], first + cc)

    for t in range(per):
        def ladder(g, _):
            x = two_rows(tbuf, 0, n, t, g)
            y = jnp.dot(kmat[...], x, preferred_element_type=F32).astype(BF16)
            lad[:, t, pl.ds(g * 32, 16), :] = y[:, :128].reshape(cols, 16, 128)
            lad[:, t, pl.ds(g * 32 + 16, 16), :] = y[:, 128:].reshape(cols, 16, 128)
            return 0

        lax.fori_loop(0, ROWS // 32, ladder, 0, unroll=8 if n <= 16 else 1)

        def start_d(k, _):
            send_d(chunk(k), t).start()
            return 0

        lax.fori_loop(1, cols, start_d, 0)
    ladr[c] = lad[c]

    def drain_n(k, _):
        peer = lax.rem(me + k, n)
        for t in range(per):
            send_t(peer, t).wait_send()
        send_a(peer).wait_send()
        return 0

    def drain_c(k, _):
        cc = chunk(k)
        for t in range(per):
            send_l(cc, t).wait_send()
        send_b(cc).wait_send()
        return 0

    def store(s):
        return pltpu.make_async_copy(amp.at[:, s], out_hbm.at[:, s], o_sem.at[s])

    def finish(cc, t):
        s = cc * per + t
        z = jnp.dot(unpack_m, ladr[cc, t], preferred_element_type=F32)
        total = lamh[s].astype(F32) + z
        d = dscr[s]
        for p in range(HELD):
            e = d - occ_ref[pairs_ref[0, p]] - occ_ref[pairs_ref[1, p]]
            q = total[p * FOLD:(p + 1) * FOLD] / e
            amp[p, s, :FOLD, :] = q[:, :64].astype(BF16)
            amp[p, s, FOLD:, :] = q[:, 64:].astype(BF16)
        store(s).start()

    for t in range(per):
        finish(c, t)
    lax.fori_loop(1, n, drain_n, 0)
    lax.fori_loop(1, cols, drain_c, 0)
    for t in range(per):
        def arrive_d(k, _):
            cc = lax.rem(c + cols - k, cols)
            rcopy(
                lad.at[cc, t], ladr.at[cc, t], d_send.at[cc, t], d_recv.at[cc, t], first + cc
            ).wait_recv()
            finish(cc, t)
            return 0

        lax.fori_loop(1, cols, arrive_d, 0)

    def drain_d(k, _):
        for t in range(per):
            send_d(chunk(k), t).wait_send()
        return 0

    lax.fori_loop(1, cols, drain_d, 0)

    def drain_out(s, _):
        store(s).wait()
        return 0

    lax.fori_loop(0, nt, drain_out, 0)


def shards(n, amplitudes, lambdas, pair_list, tile_list, occ_energy, vir_energy):
    nt = amplitudes.shape[1]
    groups = 2
    cols = n // groups
    per = nt // cols
    packed = (nt, ROWS, 128)
    dma = pltpu.SemaphoreType.DMA
    smem = pl.BlockSpec(memory_space=pltpu.SMEM)
    vmem = pl.BlockSpec(memory_space=pltpu.VMEM)
    hbm = pl.BlockSpec(memory_space=pltpu.HBM)
    return pl.pallas_call(
        functools.partial(kernel, n, groups, nt),
        out_shape=jax.ShapeDtypeStruct(lambdas.shape, BF16),
        in_specs=[smem, smem, smem, vmem, hbm, hbm],
        out_specs=pl.BlockSpec(memory_space=pl.ANY),
        scratch_shapes=[
            pltpu.VMEM(amplitudes.shape, BF16),
            pltpu.VMEM(lambdas.shape, BF16),
            pltpu.VMEM(packed, BF16),
            pltpu.VMEM(packed, BF16),
            pltpu.VMEM(packed, BF16),
            pltpu.VMEM((n, per, ROWS, 128), BF16),
            pltpu.VMEM((cols, per, ROWS, 128), BF16),
            pltpu.VMEM((cols, per, ROWS, 128), BF16),
            pltpu.VMEM((cols, per, ROWS, 128), BF16),
            pltpu.VMEM((nt, FOLD, 128), F32),
            pltpu.VMEM((n * 16, cols * 16), F32),
            pltpu.VMEM((n, HELD, cols * 16), F32),
            pltpu.VMEM((n, HELD, cols * 16), F32),
            pltpu.VMEM((HELD, n * 16), F32),
            pltpu.VMEM((cols, HELD, n * 16), F32),
            pltpu.VMEM((cols * 16, n * 16), BF16),
            dma((2, nt)),
            dma((n, per)), dma((n, per)),
            dma((cols, per)), dma((cols, per)),
            dma((n,)), dma((n,)),
            dma((cols,)), dma((cols,)),
            dma((cols, per)), dma((cols, per)),
            dma((nt,)),
        ],
        compiler_params=pltpu.CompilerParams(
            collective_id=0,
            has_side_effects=True,
            vmem_limit_bytes=61 * 2**20,
        ),
    )(tile_list.T, pair_list.T, occ_energy, vir_energy.reshape(-1, 128), amplitudes, lambdas)


def solution(mesh):
    return jax.shard_map(
        functools.partial(shards, mesh.shape["occ"]),
        mesh=mesh,
        in_specs=(
            P(("mol", "occ"), None, None, None),
            P(("mol", "occ"), None, None, None),
            P(("mol", "occ"), None),
            P(),
            P("mol"),
            P("mol"),
        ),
        out_specs=P(("mol", "occ"), None, None, None),
        check_vma=False,
    )
```

```python
import functools

import jax
import jax.numpy as jnp
from jax import lax
from jax.experimental import pallas as pl
from jax.experimental.pallas import tpu as pltpu
from jax.sharding import PartitionSpec as P

F32 = jnp.float32
BF16 = jnp.bfloat16
HELD = 8
ROWS = 256
FOLD = 32


def fold_tile(x):
    return jnp.concatenate([x[:, :FOLD, :], x[:, FOLD:, :]], axis=-1)


def kernel(
    n, groups, nt,
    tiles_ref, pairs_ref, occ_ref, vir_ref, amp_hbm, lam_hbm,
    out_hbm,
    amp, lam, pt, plam, lamh, tbuf, lbuf, ladr, dscr, gacc, asend, arecv, brecv, kmat,
    in_sem, t_send, t_recv, l_send, l_recv, a_send, a_recv, d_send, d_recv, o_sem,
):
    cols = n // groups
    per = nt // cols
    me = lax.axis_index("occ")
    c = me % cols
    first = (me // cols) * cols

    def chunk(k):
        return lax.rem(c + k, cols)

    def load(which, src, dst, s):
        return pltpu.make_async_copy(src.at[:, s], dst.at[:, s], in_sem.at[which, s])

    def load_start(k, _):
        s = chunk(k % cols) * per + k // cols
        load(0, amp_hbm, amp, s).start()
        load(1, lam_hbm, lam, s).start()
        return 0

    lax.fori_loop(0, nt, load_start, 0)

    barrier = pltpu.get_barrier_semaphore()

    def greet(k, _):
        pl.semaphore_signal(
            barrier, inc=1, device_id={"occ": lax.rem(me + k, n)}, device_id_type=pl.DeviceIdType.MESH
        )
        return 0

    lax.fori_loop(1, n, greet, 0)

    r_id = lax.broadcasted_iota(jnp.int32, (ROWS, ROWS), 0)
    m_id = lax.broadcasted_iota(jnp.int32, (ROWS, ROWS), 1)
    pack_m = ((r_id % HELD) * FOLD + r_id // HELD == m_id).astype(BF16)
    unpack_m = ((m_id % HELD) * FOLD + m_id // HELD == r_id).astype(BF16)

    def pack(s):
        load(0, amp_hbm, amp, s).wait()
        load(1, lam_hbm, lam, s).wait()
        t = fold_tile(amp[:, s]).reshape(ROWS, 2 * 64)
        pt[s] = jnp.dot(pack_m, t, preferred_element_type=F32).astype(BF16)
        u = fold_tile(lam[:, s]).reshape(ROWS, 2 * 64)
        lamh[s] = u
        plam[s] = jnp.dot(pack_m, u, preferred_element_type=F32).astype(BF16)

    def rcopy(src, dst, send, recv, peer):
        return pltpu.make_async_remote_copy(
            src_ref=src, dst_ref=dst, send_sem=send, recv_sem=recv,
            device_id={"occ": peer}, device_id_type=pl.DeviceIdType.MESH,
        )

    def send_t(peer, t):
        s = lax.rem(peer, cols) * per + t
        return rcopy(pt.at[s], tbuf.at[me, t], t_send.at[peer, t], t_recv.at[me, t], peer)

    def send_l(cc, t):
        s = cc * per + t
        return rcopy(plam.at[s], lbuf.at[c, t], l_send.at[cc, t], l_recv.at[c, t], first + cc)

    def wait_t(src, t):
        rcopy(pt.at[0], tbuf.at[src, t], t_send.at[src, t], t_recv.at[src, t], src).wait_recv()

    def wait_l(cc, t):
        rcopy(plam.at[0], lbuf.at[cc, t], l_send.at[cc, t], l_recv.at[cc, t], first + cc).wait_recv()

    pack(c * per)
    pl.semaphore_wait(barrier, n - 1)
    for t in range(per):
        if t > 0:
            pack(c * per + t)
        for g in range(1, groups):
            send_t(lax.rem(me + g * cols, n), t).start()

        def pack_send(k, _):
            cc = chunk(k)
            pack(cc * per + t)
            for g in range(groups - 1, -1, -1):
                send_t(lax.rem(first + g * cols, n) + cc, t).start()
            send_l(cc, t).start()
            return 0

        lax.fori_loop(1, cols, pack_send, 0)
    tbuf[me] = pt[pl.ds(c * per, per)]
    lbuf[c] = plam[pl.ds(c * per, per)]

    def vir_tile(i):
        row = vir_ref[pl.ds(i // 2, 1), :]
        return jnp.where(i % 2 == 0, row[:, :64], row[:, 64:])

    def energies(s, _):
        one = vir_tile(tiles_ref[0, s])
        two = vir_tile(tiles_ref[1, s])
        d = jnp.transpose(jnp.broadcast_to(one, (64, 64))) + two
        dscr[s] = jnp.concatenate([d[:FOLD], d[FOLD:]], axis=-1)
        return 0

    lax.fori_loop(0, nt, energies, 0)

    def two_rows(ref, lo, count, t, g):
        a = ref[pl.ds(lo, count), t, pl.ds(g * 32, 16), :].reshape(count * 16, 128)
        b = ref[pl.ds(lo, count), t, pl.ds(g * 32 + 16, 16), :].reshape(count * 16, 128)
        return jnp.concatenate([a, b], axis=-1)

    for t in range(per):
        def arrive_t(k, _):
            wait_t(lax.rem(me + n - k, n), t)
            return 0

        def arrive_l(k, _):
            wait_l(lax.rem(c + cols - k, cols), t)
            return 0

        lax.fori_loop(1, cols, arrive_l, 0)
        lax.fori_loop(1, n, arrive_t, 0)

        def gram(i, _):
            acc = None
            for g in range(ROWS // 32):
                x = two_rows(tbuf, i * 16, 16, t, g)
                y = two_rows(lbuf, 0, cols, t, g)
                term = lax.dot_general(x, y, (((1,), (1,)), ((), ())), preferred_element_type=F32)
                acc = term if acc is None else acc + term
            rows = pl.ds(i * 256, 256)
            gacc[rows, :] = acc if t == 0 else gacc[rows, :] + acc
            return 0

        lax.fori_loop(0, n // 16, gram, 0)

    width = cols * 16
    odd = (lax.broadcasted_iota(jnp.int32, (HELD, width), 1) // HELD) % 2

    def swap(v):
        return jnp.where(odd == 0, pltpu.roll(v, width - HELD, 1), pltpu.roll(v, HELD, 1))

    def block(i):
        v = jnp.where(odd == 0, gacc[pl.ds(i * 16, HELD), :], gacc[pl.ds(i * 16 + HELD, HELD), :])
        return v + swap(v)

    for g in range(groups):
        def fold_gram(m, _):
            i = g * cols + 4 * m
            v = jnp.concatenate(
                [jnp.where(odd == 0, block(i + j), block(i + j + 1)) for j in (0, 2)], axis=0
            )
            asend[g, pl.ds(m * 16, 16), :] = v.astype(BF16)
            return 0

        lax.fori_loop(0, cols // 4, fold_gram, 0, unroll=2)

    def send_a(peer):
        return rcopy(asend.at[peer // cols], arecv.at[me], a_send.at[peer], a_recv.at[me], peer)

    def start_a(k, _):
        send_a(lax.rem(me + k, n)).start()
        return 0

    lax.fori_loop(1, n, start_a, 0)
    arecv[me] = asend[me // cols]

    def arrive_a(k, _):
        src = lax.rem(me + n - k, n)
        rcopy(asend.at[0], arecv.at[src], a_send.at[src], a_recv.at[src], src).wait_recv()
        return 0

    lax.fori_loop(1, n, arrive_a, 0)
    for g in range(groups):
        lanes = slice(g * width, (g + 1) * width)
        total = arecv[g * cols].astype(F32)
        for i in range(1, cols):
            total = total + arecv[g * cols + i].astype(F32)
        total = 0.5 * total.astype(BF16).astype(F32)
        for j in range(cols // 2):
            v = total[j * HELD:(j + 1) * HELD]
            w = swap(v)
            brecv[2 * j, :, lanes] = jnp.where(odd == 0, v, w)
            brecv[2 * j + 1, :, lanes] = jnp.where(odd == 0, w, v)

    all_odd = (lax.broadcasted_iota(jnp.int32, (HELD, n * 16), 1) // HELD) % 2

    def expand(i, _):
        rows = brecv[i]
        both = jnp.concatenate(
            [jnp.where(all_odd == 0, rows, 0.0), jnp.where(all_odd == 1, rows, 0.0)], axis=0
        )
        kmat[pl.ds(i * 16, 16), :] = both.astype(BF16)
        return 0

    lax.fori_loop(0, cols, expand, 0, unroll=8)

    lad = lbuf

    def send_d(cc, t):
        return rcopy(lad.at[cc, t], ladr.at[c, t], d_send.at[cc, t], d_recv.at[c, t], first + cc)

    for t in range(per):
        def ladder(g, _):
            x = two_rows(tbuf, 0, n, t, g)
            y = jnp.dot(kmat[...], x, preferred_element_type=F32).astype(BF16)
            lad[:, t, pl.ds(g * 32, 16), :] = y[:, :128].reshape(cols, 16, 128)
            lad[:, t, pl.ds(g * 32 + 16, 16), :] = y[:, 128:].reshape(cols, 16, 128)
            return 0

        lax.fori_loop(0, ROWS // 32, ladder, 0, unroll=8 if n <= 16 else 1)

        def start_d(k, _):
            send_d(chunk(k), t).start()
            return 0

        lax.fori_loop(1, cols, start_d, 0)
    ladr[c] = lad[c]

    def drain_n(k, _):
        peer = lax.rem(me + k, n)
        for t in range(per):
            send_t(peer, t).wait_send()
        send_a(peer).wait_send()
        return 0

    def drain_c(k, _):
        cc = chunk(k)
        for t in range(per):
            send_l(cc, t).wait_send()
        return 0

    def store(s):
        return pltpu.make_async_copy(amp.at[:, s], out_hbm.at[:, s], o_sem.at[s])

    def finish(cc, t):
        s = cc * per + t
        z = jnp.dot(unpack_m, ladr[cc, t], preferred_element_type=F32)
        total = lamh[s].astype(F32) + z
        d = dscr[s]
        for p in range(HELD):
            e = d - occ_ref[pairs_ref[0, p]] - occ_ref[pairs_ref[1, p]]
            q = total[p * FOLD:(p + 1) * FOLD] / e
            amp[p, s, :FOLD, :] = q[:, :64].astype(BF16)
            amp[p, s, FOLD:, :] = q[:, 64:].astype(BF16)
        store(s).start()

    for t in range(per):
        finish(c, t)
    lax.fori_loop(1, n, drain_n, 0)
    lax.fori_loop(1, cols, drain_c, 0)
    for t in range(per):
        def arrive_d(k, _):
            cc = lax.rem(c + cols - k, cols)
            rcopy(
                lad.at[cc, t], ladr.at[cc, t], d_send.at[cc, t], d_recv.at[cc, t], first + cc
            ).wait_recv()
            finish(cc, t)
            return 0

        lax.fori_loop(1, cols, arrive_d, 0)

    def drain_d(k, _):
        for t in range(per):
            send_d(chunk(k), t).wait_send()
        return 0

    lax.fori_loop(1, cols, drain_d, 0)

    def drain_out(s, _):
        store(s).wait()
        return 0

    lax.fori_loop(0, nt, drain_out, 0)


def shards(n, amplitudes, lambdas, pair_list, tile_list, occ_energy, vir_energy):
    nt = amplitudes.shape[1]
    groups = 2
    cols = n // groups
    per = nt // cols
    packed = (nt, ROWS, 128)
    dma = pltpu.SemaphoreType.DMA
    smem = pl.BlockSpec(memory_space=pltpu.SMEM)
    vmem = pl.BlockSpec(memory_space=pltpu.VMEM)
    hbm = pl.BlockSpec(memory_space=pltpu.HBM)
    return pl.pallas_call(
        functools.partial(kernel, n, groups, nt),
        out_shape=jax.ShapeDtypeStruct(lambdas.shape, BF16),
        in_specs=[smem, smem, smem, vmem, hbm, hbm],
        out_specs=pl.BlockSpec(memory_space=pl.ANY),
        scratch_shapes=[
            pltpu.VMEM(amplitudes.shape, BF16),
            pltpu.VMEM(lambdas.shape, BF16),
            pltpu.VMEM(packed, BF16),
            pltpu.VMEM(packed, BF16),
            pltpu.VMEM(packed, BF16),
            pltpu.VMEM((n, per, ROWS, 128), BF16),
            pltpu.VMEM((cols, per, ROWS, 128), BF16),
            pltpu.VMEM((cols, per, ROWS, 128), BF16),
            pltpu.VMEM((nt, FOLD, 128), F32),
            pltpu.VMEM((n * 16, cols * 16), F32),
            pltpu.VMEM((groups, cols * 4, cols * 16), BF16),
            pltpu.VMEM((n, cols * 4, cols * 16), BF16),
            pltpu.VMEM((cols, HELD, n * 16), F32),
            pltpu.VMEM((cols * 16, n * 16), BF16),
            dma((2, nt)),
            dma((n, per)), dma((n, per)),
            dma((cols, per)), dma((cols, per)),
            dma((n,)), dma((n,)),
            dma((cols, per)), dma((cols, per)),
            dma((nt,)),
        ],
        compiler_params=pltpu.CompilerParams(
            collective_id=0,
            has_side_effects=True,
            vmem_limit_bytes=61 * 2**20,
        ),
    )(tile_list.T, pair_list.T, occ_energy, vir_energy.reshape(-1, 128), amplitudes, lambdas)


def solution(mesh):
    return jax.shard_map(
        functools.partial(shards, mesh.shape["occ"]),
        mesh=mesh,
        in_specs=(
            P(("mol", "occ"), None, None, None),
            P(("mol", "occ"), None, None, None),
            P(("mol", "occ"), None),
            P(),
            P("mol"),
            P("mol"),
        ),
        out_specs=P(("mol", "occ"), None, None, None),
        check_vma=False,
    )
```

```python
import functools

import jax
import jax.numpy as jnp
from jax import lax
from jax.experimental import pallas as pl
from jax.experimental.pallas import tpu as pltpu
from jax.sharding import PartitionSpec as P

F32 = jnp.float32
BF16 = jnp.bfloat16
HELD = 8
ROWS = 256
FOLD = 32


def fold_tile(x):
    return jnp.concatenate([x[:, :FOLD, :], x[:, FOLD:, :]], axis=-1)


def kernel(
    n, groups, nt,
    tiles_hbm, pairs_hbm, occ_hbm, vir_hbm, amp_hbm, lam_hbm,
    out_hbm,
    amp, lam, pt, plam, lamh, tbuf, lbuf, ladr, dscr, gacc, asend, arecv, brecv, kmat,
    in_sem, t_send, t_recv, l_send, l_recv, a_send, a_recv, d_send, d_recv, o_sem,
    tiles_ref, pairs_ref, occ_ref, vir_ref, table_sem,
):
    cols = n // groups
    per = nt // cols
    me = lax.axis_index("occ")
    c = me % cols
    first = (me // cols) * cols

    def chunk(k):
        return lax.rem(c + k, cols)

    def load(which, src, dst, s):
        return pltpu.make_async_copy(src.at[:, s], dst.at[:, s], in_sem.at[which, s])

    def load_start(k, _):
        s = chunk(k % cols) * per + k // cols
        load(0, amp_hbm, amp, s).start()
        load(1, lam_hbm, lam, s).start()
        return 0

    lax.fori_loop(0, nt, load_start, 0)
    tables = [
        pltpu.make_async_copy(src, dst, table_sem.at[i])
        for i, (src, dst) in enumerate(
            [(tiles_hbm, tiles_ref), (pairs_hbm, pairs_ref), (occ_hbm, occ_ref), (vir_hbm, vir_ref)]
        )
    ]
    for copy in tables:
        copy.start()

    barrier = pltpu.get_barrier_semaphore()

    def greet(k, _):
        pl.semaphore_signal(
            barrier, inc=1, device_id={"occ": lax.rem(me + k, n)}, device_id_type=pl.DeviceIdType.MESH
        )
        return 0

    lax.fori_loop(1, n, greet, 0)

    r_id = lax.broadcasted_iota(jnp.int32, (ROWS, ROWS), 0)
    m_id = lax.broadcasted_iota(jnp.int32, (ROWS, ROWS), 1)
    pack_m = ((r_id % HELD) * FOLD + r_id // HELD == m_id).astype(BF16)
    unpack_m = ((m_id % HELD) * FOLD + m_id // HELD == r_id).astype(BF16)

    def pack(s):
        load(0, amp_hbm, amp, s).wait()
        load(1, lam_hbm, lam, s).wait()
        t = fold_tile(amp[:, s]).reshape(ROWS, 2 * 64)
        pt[s] = jnp.dot(pack_m, t, preferred_element_type=F32).astype(BF16)
        u = fold_tile(lam[:, s]).reshape(ROWS, 2 * 64)
        lamh[s] = u
        plam[s] = jnp.dot(pack_m, u, preferred_element_type=F32).astype(BF16)

    def rcopy(src, dst, send, recv, peer):
        return pltpu.make_async_remote_copy(
            src_ref=src, dst_ref=dst, send_sem=send, recv_sem=recv,
            device_id={"occ": peer}, device_id_type=pl.DeviceIdType.MESH,
        )

    def send_t(peer, t):
        s = lax.rem(peer, cols) * per + t
        return rcopy(pt.at[s], tbuf.at[me, t], t_send.at[peer, t], t_recv.at[me, t], peer)

    def send_l(cc, t):
        s = cc * per + t
        return rcopy(plam.at[s], lbuf.at[c, t], l_send.at[cc, t], l_recv.at[c, t], first + cc)

    def wait_t(src, t):
        rcopy(pt.at[0], tbuf.at[src, t], t_send.at[src, t], t_recv.at[src, t], src).wait_recv()

    def wait_l(cc, t):
        rcopy(plam.at[0], lbuf.at[cc, t], l_send.at[cc, t], l_recv.at[cc, t], first + cc).wait_recv()

    pack(c * per)
    pl.semaphore_wait(barrier, n - 1)
    for t in range(per):
        if t > 0:
            pack(c * per + t)
        for g in range(1, groups):
            send_t(lax.rem(me + g * cols, n), t).start()

        def pack_send(k, _):
            cc = chunk(k)
            pack(cc * per + t)
            for g in range(groups - 1, -1, -1):
                send_t(lax.rem(first + g * cols, n) + cc, t).start()
            send_l(cc, t).start()
            return 0

        lax.fori_loop(1, cols, pack_send, 0)
    tbuf[me] = pt[pl.ds(c * per, per)]
    lbuf[c] = plam[pl.ds(c * per, per)]

    def vir_tile(i):
        row = vir_ref[pl.ds(i // 2, 1), :]
        return jnp.where(i % 2 == 0, row[:, :64], row[:, 64:])

    def energies(s, _):
        one = vir_tile(tiles_ref[0, s])
        two = vir_tile(tiles_ref[1, s])
        d = jnp.transpose(jnp.broadcast_to(one, (64, 64))) + two
        dscr[s] = jnp.concatenate([d[:FOLD], d[FOLD:]], axis=-1)
        return 0

    for copy in tables:
        copy.wait()
    lax.fori_loop(0, nt, energies, 0)

    def two_rows(ref, lo, count, t, g):
        a = ref[pl.ds(lo, count), t, pl.ds(g * 32, 16), :].reshape(count * 16, 128)
        b = ref[pl.ds(lo, count), t, pl.ds(g * 32 + 16, 16), :].reshape(count * 16, 128)
        return jnp.concatenate([a, b], axis=-1)

    for t in range(per):
        def arrive_t(k, _):
            wait_t(lax.rem(me + n - k, n), t)
            return 0

        def arrive_l(k, _):
            wait_l(lax.rem(c + cols - k, cols), t)
            return 0

        lax.fori_loop(1, cols, arrive_l, 0)
        lax.fori_loop(1, n, arrive_t, 0)

        def gram(i, _):
            acc = None
            for g in range(ROWS // 32):
                x = two_rows(tbuf, i * 16, 16, t, g)
                y = two_rows(lbuf, 0, cols, t, g)
                term = lax.dot_general(x, y, (((1,), (1,)), ((), ())), preferred_element_type=F32)
                acc = term if acc is None else acc + term
            rows = pl.ds(i * 256, 256)
            gacc[rows, :] = acc if t == 0 else gacc[rows, :] + acc
            return 0

        lax.fori_loop(0, n // 16, gram, 0)

    width = cols * 16
    odd = (lax.broadcasted_iota(jnp.int32, (HELD, width), 1) // HELD) % 2

    def swap(v):
        return jnp.where(odd == 0, pltpu.roll(v, width - HELD, 1), pltpu.roll(v, HELD, 1))

    def block(i):
        v = jnp.where(odd == 0, gacc[pl.ds(i * 16, HELD), :], gacc[pl.ds(i * 16 + HELD, HELD), :])
        return v + swap(v)

    for g in range(groups):
        def fold_gram(m, _):
            i = g * cols + 4 * m
            v = jnp.concatenate(
                [jnp.where(odd == 0, block(i + j), block(i + j + 1)) for j in (0, 2)], axis=0
            )
            asend[g, pl.ds(m * 16, 16), :] = v.astype(BF16)
            return 0

        lax.fori_loop(0, cols // 4, fold_gram, 0, unroll=2)

    def send_a(peer):
        return rcopy(asend.at[peer // cols], arecv.at[me], a_send.at[peer], a_recv.at[me], peer)

    def start_a(k, _):
        send_a(lax.rem(me + k, n)).start()
        return 0

    lax.fori_loop(1, n, start_a, 0)
    arecv[me] = asend[me // cols]

    def arrive_a(k, _):
        src = lax.rem(me + n - k, n)
        rcopy(asend.at[0], arecv.at[src], a_send.at[src], a_recv.at[src], src).wait_recv()
        return 0

    lax.fori_loop(1, n, arrive_a, 0)
    for g in range(groups):
        lanes = slice(g * width, (g + 1) * width)
        total = arecv[g * cols].astype(F32)
        for i in range(1, cols):
            total = total + arecv[g * cols + i].astype(F32)
        total = 0.5 * total.astype(BF16).astype(F32)
        for j in range(cols // 2):
            v = total[j * HELD:(j + 1) * HELD]
            w = swap(v)
            brecv[2 * j, :, lanes] = jnp.where(odd == 0, v, w)
            brecv[2 * j + 1, :, lanes] = jnp.where(odd == 0, w, v)

    all_odd = (lax.broadcasted_iota(jnp.int32, (HELD, n * 16), 1) // HELD) % 2

    def expand(i, _):
        rows = brecv[i]
        both = jnp.concatenate(
            [jnp.where(all_odd == 0, rows, 0.0), jnp.where(all_odd == 1, rows, 0.0)], axis=0
        )
        kmat[pl.ds(i * 16, 16), :] = both.astype(BF16)
        return 0

    lax.fori_loop(0, cols, expand, 0, unroll=8)

    lad = lbuf

    def send_d(cc, t):
        return rcopy(lad.at[cc, t], ladr.at[c, t], d_send.at[cc, t], d_recv.at[c, t], first + cc)

    for t in range(per):
        def ladder(g, _):
            x = two_rows(tbuf, 0, n, t, g)
            y = jnp.dot(kmat[...], x, preferred_element_type=F32).astype(BF16)
            lad[:, t, pl.ds(g * 32, 16), :] = y[:, :128].reshape(cols, 16, 128)
            lad[:, t, pl.ds(g * 32 + 16, 16), :] = y[:, 128:].reshape(cols, 16, 128)
            return 0

        lax.fori_loop(0, ROWS // 32, ladder, 0, unroll=8 if n <= 16 else 1)

        def start_d(k, _):
            send_d(chunk(k), t).start()
            return 0

        lax.fori_loop(1, cols, start_d, 0)
    ladr[c] = lad[c]

    def drain_n(k, _):
        peer = lax.rem(me + k, n)
        for t in range(per):
            send_t(peer, t).wait_send()
        send_a(peer).wait_send()
        return 0

    def drain_c(k, _):
        cc = chunk(k)
        for t in range(per):
            send_l(cc, t).wait_send()
        return 0

    def store(s):
        return pltpu.make_async_copy(amp.at[:, s], out_hbm.at[:, s], o_sem.at[s])

    def finish(cc, t):
        s = cc * per + t
        z = jnp.dot(unpack_m, ladr[cc, t], preferred_element_type=F32)
        total = lamh[s].astype(F32) + z
        d = dscr[s]
        for p in range(HELD):
            e = d - occ_ref[pairs_ref[0, p]] - occ_ref[pairs_ref[1, p]]
            q = total[p * FOLD:(p + 1) * FOLD] / e
            amp[p, s, :FOLD, :] = q[:, :64].astype(BF16)
            amp[p, s, FOLD:, :] = q[:, 64:].astype(BF16)
        store(s).start()

    for t in range(per):
        finish(c, t)
    lax.fori_loop(1, n, drain_n, 0)
    lax.fori_loop(1, cols, drain_c, 0)
    for t in range(per):
        def arrive_d(k, _):
            cc = lax.rem(c + cols - k, cols)
            rcopy(
                lad.at[cc, t], ladr.at[cc, t], d_send.at[cc, t], d_recv.at[cc, t], first + cc
            ).wait_recv()
            finish(cc, t)
            return 0

        lax.fori_loop(1, cols, arrive_d, 0)

    def drain_d(k, _):
        for t in range(per):
            send_d(chunk(k), t).wait_send()
        return 0

    lax.fori_loop(1, cols, drain_d, 0)

    def drain_out(s, _):
        store(s).wait()
        return 0

    lax.fori_loop(0, nt, drain_out, 0)


def shards(n, amplitudes, lambdas, pair_list, tile_list, occ_energy, vir_energy):
    nt = amplitudes.shape[1]
    groups = 2
    cols = n // groups
    per = nt // cols
    packed = (nt, ROWS, 128)
    dma = pltpu.SemaphoreType.DMA
    hbm = pl.BlockSpec(memory_space=pltpu.HBM)
    return pl.pallas_call(
        functools.partial(kernel, n, groups, nt),
        out_shape=jax.ShapeDtypeStruct(lambdas.shape, BF16),
        in_specs=[hbm] * 6,
        out_specs=pl.BlockSpec(memory_space=pl.ANY),
        scratch_shapes=[
            pltpu.VMEM(amplitudes.shape, BF16),
            pltpu.VMEM(lambdas.shape, BF16),
            pltpu.VMEM(packed, BF16),
            pltpu.VMEM(packed, BF16),
            pltpu.VMEM(packed, BF16),
            pltpu.VMEM((n, per, ROWS, 128), BF16),
            pltpu.VMEM((cols, per, ROWS, 128), BF16),
            pltpu.VMEM((cols, per, ROWS, 128), BF16),
            pltpu.VMEM((nt, FOLD, 128), F32),
            pltpu.VMEM((n * 16, cols * 16), F32),
            pltpu.VMEM((groups, cols * 4, cols * 16), BF16),
            pltpu.VMEM((n, cols * 4, cols * 16), BF16),
            pltpu.VMEM((cols, HELD, n * 16), F32),
            pltpu.VMEM((cols * 16, n * 16), BF16),
            dma((2, nt)),
            dma((n, per)), dma((n, per)),
            dma((cols, per)), dma((cols, per)),
            dma((n,)), dma((n,)),
            dma((cols, per)), dma((cols, per)),
            dma((nt,)),
            pltpu.SMEM(tile_list.shape[::-1], jnp.int32),
            pltpu.SMEM(pair_list.shape[::-1], jnp.int32),
            pltpu.SMEM(occ_energy.shape, F32),
            pltpu.VMEM((vir_energy.shape[0] // 128, 128), F32),
            dma((4,)),
        ],
        compiler_params=pltpu.CompilerParams(
            collective_id=0,
            has_side_effects=True,
            vmem_limit_bytes=61 * 2**20,
        ),
    )(tile_list.T, pair_list.T, occ_energy, vir_energy.reshape(-1, 128), amplitudes, lambdas)


def solution(mesh):
    return jax.shard_map(
        functools.partial(shards, mesh.shape["occ"]),
        mesh=mesh,
        in_specs=(
            P(("mol", "occ"), None, None, None),
            P(("mol", "occ"), None, None, None),
            P(("mol", "occ"), None),
            P(),
            P("mol"),
            P("mol"),
        ),
        out_specs=P(("mol", "occ"), None, None, None),
        check_vma=False,
    )
```
